128 devices in a mesh: cent: 16 (over y, z_lo, core), dp: 8 (over x, z_hi).
Axes of the slice: x: 4, y: 4, z: 4 (z_hi: 2, z_lo: 2; z = z_hi * 2 + z_lo), core: 2. Of those that a mesh axis runs over, the one named last changes fastest.
Arguments:
- images: bfloat16 [4096, 1536], P('dp')
- cents: bfloat16 [16384, 1536], P('cent')
- tops: bfloat16 [8192, 1536], P('dp')
Outputs:
- level_one: bfloat16 [16384, 1536], P(('cent', 'dp'))
- level_two: bfloat16 [8, 1024, 1536], P('dp', 'cent')
All inputs are finite; a program needn't handle non-finite values.
Results may differ from the reference program's by a relative error of at most 0.007.
Values may be sent and summed in bfloat16 or wider, within the bound.
A program may use at most 64 MiB of HBM per device.

```python
import math
import jax
import jax.numpy as jnp
from jax import lax

D = 1536
IMG_DEV = 512
K2_DEV = 1024
NI = 4096
K1 = 16384
K2 = 8192
N_DP = 8


def shared_base(key):
    return jax.random.normal(key, (K1, D), jnp.float32)


def drawn_rows():
    marks = jnp.arange(4 * (NI // IMG_DEV), dtype=jnp.int32)
    rows = marks // 4 * IMG_DEV + marks % 4
    pick = rows * 7919 % K1
    other = (pick + 1) % K1
    return (marks, rows, pick, other)


def cent_gain():
    return (160.0 / D ** 0.5) ** 0.5


def draw_cents(key, part):
    base = shared_base(key)
    marks, rows, pick, other = drawn_rows()
    flagged = jnp.zeros((K1,), jnp.float32).at[pick].set(1.0).at[other].set(1.0)
    lifted = base * (1.0 + (cent_gain() - 1.0) * flagged)[:, None]
    return lifted.astype(jnp.bfloat16)


def draw_images(key, part):
    base = shared_base(key)
    key = jax.random.fold_in(key, 7)
    first, second = jax.random.split(key)
    marks, rows, pick, other = drawn_rows()
    strength = 100.0 + 120.0 * jax.random.uniform(second, (rows.shape[0], 1), jnp.float32)
    gain = strength / (D ** 0.5 * cent_gain())
    aligned = gain * (base[pick] + base[other])
    noise = jax.random.normal(first, (NI, D), jnp.float32)
    return noise.at[rows].set(aligned).astype(jnp.bfloat16)


def draw_tops(key, part):
    base = shared_base(key)
    key = jax.random.fold_in(key, 11)
    marks, rows, pick, other = drawn_rows()
    leading = 0.875 * cent_gain() * (base[pick] + base[other])
    trailing = 0.99 * leading
    slots = marks * (K2 // marks.shape[0])
    noise = jnp.clip(jax.random.normal(key, (K2, D), jnp.float32), -6.0, 6.0)
    noise = noise.at[slots].set(leading)
    noise = noise.at[slots + 1].set(trailing)
    return noise.astype(jnp.bfloat16)


def setup_inputs(seed: int = 0) -> dict:
    keys = jax.random.split(jax.random.key(seed), 4)
    images = draw_images(jax.random.fold_in(keys[3], 71), 0)
    cents = draw_cents(jax.random.fold_in(keys[3], 71), 0)
    tops = draw_tops(jax.random.fold_in(keys[3], 71), 0)
    return {"images": images, "cents": cents, "tops": tops}


prior = 0.1


def cluster(data, centers, rows_block):
    width = data.shape[1]
    scale = width ** -0.5
    count = centers.shape[0]
    blocks = data.reshape(-1, rows_block, width)

    def step(carry, block):
        moved, mass = carry
        scores = jnp.dot(block, centers.T, preferred_element_type=jnp.float32) * scale
        peak = jnp.max(scores, axis=1, keepdims=True)
        expo = jnp.exp(scores - peak)
        resp = expo / jnp.sum(expo, axis=1, keepdims=True)
        moved = moved + jnp.dot(resp.astype(jnp.bfloat16).T, block, preferred_element_type=jnp.float32)
        mass = mass + jnp.sum(resp, axis=0)
        return (moved, mass), None

    start = (jnp.zeros((count, width), jnp.float32), jnp.zeros((count,), jnp.float32))
    (moved, mass), _ = lax.scan(step, start, blocks)
    updated = (moved + prior * centers.astype(jnp.float32)) / (mass + prior)[:, None]
    return updated.astype(jnp.bfloat16)


def reference(images, cents, tops):
    level_one = cluster(images, cents, math.gcd(1024, images.shape[0]))
    updated = cluster(level_one, tops, math.gcd(1024, level_one.shape[0]))
    return level_one, updated.reshape(N_DP, K2_DEV, D)
```

```python
import jax
import jax.numpy as jnp
from jax import lax
from jax.experimental import pallas as pl
from jax.experimental.pallas import tpu as pltpu
from jax.sharding import PartitionSpec as P

prior = 0.1
MESH = pl.DeviceIdType.MESH
f32, bf16 = jnp.float32, jnp.bfloat16
NT = (((1,), (1,)), ((), ()))
NN = (((1,), (0,)), ((), ()))
D = 1536
SHARD = 512
ROWS = 1024
NX = (256, 128)
NQ = ((SHARD - NX[0]) // 4, (SHARD - NX[1]) // 4)
HX = (NX[0] // 2, NX[1] // 2)
HQ = (NQ[0] // 2, NQ[1] // 2)
KAPPA = D ** -0.5 * 1.4426950408889634
ORDER = (1, 3, 2)


def xor4(v, r):
    if r == 0:
        return v
    if r == 1:
        return v + 1 - 2 * lax.rem(v, 2)
    if r == 2:
        return lax.rem(v + 2, 4)
    return 3 - v


def flip(v, r):
    return 1 - v if r else v


def kernel(images, cents, tops, out1, out2,
           img, ce, to, S, Pb, acc, mass, data, stat, stat2, msum, dsend, drecv, snd, rcv,
           gs, gr, ss, sr, s2s, s2r, mss, msr, ds, dr, rs, rr, ld):
    ci = lax.axis_index("cent")
    di = lax.axis_index("dp")
    y, zl, c = lax.div(ci, 4), lax.rem(lax.div(ci, 2), 2), lax.rem(ci, 2)
    x, zh = lax.div(di, 2), lax.rem(di, 2)

    def dev(x, y, zh, zl, c):
        return ((y * 2 + zl) * 2 + c, x * 2 + zh)

    def centpeer(r):
        return dev(x, xor4(y, r // 4), zh, flip(zl, (r // 2) % 2), flip(c, r % 2))

    def dppeer(r):
        return dev(xor4(x, r // 2), y, flip(zh, r % 2), zl, c)

    partner = centpeer(1)
    zpeer = dev(x, y, 1 - zh, 1 - zl, c)

    l_img = pltpu.make_async_copy(images, img.at[0, 0], ld.at[0])
    l_ce = pltpu.make_async_copy(cents, ce, ld.at[1])
    l_img.start()
    l_ce.start()
    l_to = []
    for b in range(16):
        yy, zz, cc = b // 4, (b // 2) % 2, b % 2
        pos = cc * 512 + yy * 128 + zz * 64
        l_to.append(pltpu.make_async_copy(tops.at[pl.ds(b * 64, 64)], to.at[pl.ds(pos, 64)], ld.at[2 + b]))

    barrier = pltpu.get_barrier_semaphore()
    everyone = [centpeer(r) for r in range(1, 16)] + [dppeer(r) for r in range(1, 8)] + [zpeer]
    for p in everyone:
        pl.semaphore_signal(barrier, inc=1, device_id=p, device_id_type=MESH)
    pl.semaphore_wait(barrier, len(everyone))

    names = {}

    def copy(name, src, dst, device):
        i = len(names)
        names[name] = pltpu.make_async_remote_copy(
            src_ref=src, dst_ref=dst, send_sem=gs.at[i], recv_sem=gr.at[i],
            device_id=device, device_id_type=MESH)

    def rx(z, core):
        return pl.ds(pl.multiple_of(core * HX[z], HX[z]), HX[z])

    def rq(z, q, core):
        return pl.ds(pl.multiple_of(NX[z] + q * NQ[z] + core * HQ[z], 16), HQ[z])

    copy("zx", img.at[0, 0, rx(1, c)], img.at[1, 0, rx(1, c)], zpeer)
    for k in range(4):
        rows = rq(1, xor4(y, k), c)
        copy(("zq", k), img.at[0, 0, rows], img.at[1, 0, rows], zpeer)
    for z in range(2):
        for r in ORDER:
            device = dev(xor4(x, r), y, zh, zl, c)
            copy(("xq", z, r), img.at[z, 0, rq(z, y, c)], img.at[z, r, rq(z, y, c)], device)
            copy(("xx", z, r), img.at[z, 0, rx(z, c)], img.at[z, r, rx(z, c)], device)
        for r in ORDER:
            device = dev(x, xor4(y, r), zh, zl, c)
            rows = rq(z, y, c)
            copy(("yq", z, r), img.at[z, pl.ds(1, 3), rows], img.at[z, pl.ds(1, 3), rows], device)
    copy("dzx", img.at[1, 0, rx(1, c)], img.at[1, 0, rx(1, c)], partner)
    for k in range(4):
        rows = rq(1, xor4(y, k), c)
        copy(("dzq", k), img.at[1, 0, rows], img.at[1, 0, rows], partner)
    for z in range(2):
        for r in ORDER:
            copy(("dxx", z, r), img.at[z, r, rx(z, c)], img.at[z, r, rx(z, c)], partner)
        rows = rq(z, y, c)
        copy(("dxq", z), img.at[z, pl.ds(1, 3), rows], img.at[z, pl.ds(1, 3), rows], partner)
        for r in ORDER:
            rows = rq(z, xor4(y, r), c)
            copy(("dyq", z, r), img.at[z, pl.ds(1, 3), rows], img.at[z, pl.ds(1, 3), rows], partner)

    def start(*ns):
        for n in ns:
            names[n].start()

    def arrive(*ns):
        for n in ns:
            names[n].wait_recv()

    def relay(*pairs):
        for n, m in pairs:
            arrive(n)
            start(m)

    l_img.wait()
    start(*[("xq", 0, r) for r in ORDER])
    start("zx", ("zq", 0))
    start(("xx", 0, 1), ("xx", 0, 3))
    start(("zq", 1), ("zq", 3), ("zq", 2))
    start(("xx", 0, 2))
    for l in l_to:
        l.start()
    l_ce.wait()

    mass[...] = jnp.zeros_like(mass)
    acc[...] = jnp.zeros_like(acc)

    def softmax_pass(sl, cols):
        m = jnp.max(S[sl], axis=0, keepdims=True)

        def tile(j, l):
            rows = pl.ds(pl.multiple_of(j * 128, 128), 128)
            e = jnp.exp2((S[sl, rows, :] - m) * KAPPA)
            S[sl, rows, :] = e
            return l + jnp.sum(e.reshape(16, 8, cols), axis=0)

        l = lax.fori_loop(0, ROWS // 128, tile, jnp.zeros((8, cols), f32))
        return m, jnp.sum(l, axis=0, keepdims=True)

    def stat_copies(buf, j, count, ssem, rsem, peer):
        return [pltpu.make_async_remote_copy(
            src_ref=buf.at[j, 0], dst_ref=buf.at[j, r], send_sem=ssem.at[j], recv_sem=rsem.at[j],
            device_id=peer(r), device_id_type=MESH) for r in range(1, count)]

    def scores_chunk(j, z, xr):
        sl = j % 2
        for n in range(2):
            cols = slice(n * 256, (n + 1) * 256)
            S[sl, :, cols] = lax.dot_general(ce[...], img[z, xr, cols, :], NT, preferred_element_type=f32)
        m, l = softmax_pass(sl, 512)
        stat[j, 0, 0:1, :] = m
        stat[j, 0, 1:2, :] = l
        for cp in stat_copies(stat, j, 16, ss, sr, centpeer):
            cp.start()

    def combine(buf, j, count):
        ms = [buf[j, r, 0:1, :] for r in range(count)]
        M = ms[0]
        for v in ms[1:]:
            M = jnp.maximum(M, v)
        L = jnp.zeros_like(M)
        for r in range(count):
            L = L + buf[j, r, 1:2, :] * jnp.exp2((ms[r] - M) * KAPPA)
        return jnp.exp2((ms[0] - M) * KAPPA) / L

    def wait_bytes(ref, sem):
        pltpu.make_async_copy(ref, ref, sem).wait()

    def weights(sl, f, c0, cols):
        @pl.loop(0, ROWS // 128)
        def _(t):
            rows = pl.ds(pl.multiple_of(t * 128, 128), 128)
            p = S[sl, rows, :] * f
            Pb[rows, c0:c0 + cols] = p.astype(bf16)
            q = p[:, 0:128]
            for i in range(1, cols // 128):
                q = q + p[:, i * 128:(i + 1) * 128]
            mass[rows, :] += q

    def moved_chunk(j, z, xr):
        sl = j % 2
        wait_bytes(stat.at[j, pl.ds(1, 15)], sr.at[j])
        f = combine(stat, j, 16)
        weights(sl, f, 0, 512)

        @pl.loop(0, 2)
        def _(t):
            rows = pl.ds(pl.multiple_of(t * 512, 512), 512)
            p = Pb[rows, 0:512]
            for d in range(3):
                cols = slice(d * 512, (d + 1) * 512)
                acc[rows, cols] += lax.dot_general(p, img[z, xr, :, cols], NN, preferred_element_type=f32)

    def ygo(z):
        arrive(*[("xq", z, r) for r in ORDER])
        start(*[("yq", z, r) for r in ORDER], ("dxq", z))

    def xgo1():
        relay(("zx", "dzx"), (("zq", 0), ("dzq", 0)))
        start(*[("xq", 1, r) for r in ORDER])
        start(*[("xx", 1, r) for r in ORDER])

    seq = [(0, 0), (0, 1), (0, 3), (1, 0), (0, 2), (1, 1), (1, 3), (1, 2)]

    scores_chunk(0, 0, 0)
    ygo(0)
    xgo1()
    moved_chunk(0, 0, 0)
    relay((("xx", 0, 1), ("dxx", 0, 1)), (("xx", 0, 3), ("dxx", 0, 3)))
    relay(*[(("yq", 0, r), ("dyq", 0, r)) for r in ORDER])
    arrive(("dxx", 0, 1), ("dxq", 0), *[("dyq", 0, r) for r in ORDER])
    scores_chunk(1, 0, 1)
    ygo(1)
    arrive(("dxx", 0, 3))
    scores_after = {}
    for j in range(1, 8):
        z, xr = seq[j]
        if j + 1 < 8:
            nz, nx = seq[j + 1]
            if (nz, nx) == (1, 0):
                relay(*[(("zq", k), ("dzq", k)) for k in (1, 3, 2)])
                arrive("dzx", *[("dzq", k) for k in range(4)])
            if (nz, nx) == (0, 2):
                relay((("xx", 0, 2), ("dxx", 0, 2)))
                arrive(("dxx", 0, 2))
            if (nz, nx) == (1, 1):
                relay(*[(("xx", 1, r), ("dxx", 1, r)) for r in (1, 3)])
                relay(*[(("yq", 1, r), ("dyq", 1, r)) for r in ORDER])
                arrive(("dxx", 1, 1), ("dxx", 1, 3), ("dxq", 1), *[("dyq", 1, r) for r in ORDER])
            if (nz, nx) == (1, 2):
                relay((("xx", 1, 2), ("dxx", 1, 2)))
                arrive(("dxx", 1, 2))
            scores_chunk(j + 1, nz, nx)
        moved_chunk(j, z, xr)

    inv = 1.0 / (jnp.sum(mass[...], axis=1, keepdims=True) + prior)
    data[...] = ((acc[...] + prior * ce[...].astype(f32)) * inv).astype(bf16)
    o1 = pltpu.make_async_copy(data.at[pl.ds(pl.multiple_of(di * 128, 128), 128)], out1, ld.at[0])
    o1.start()

    for l in l_to:
        l.wait()
    mass[...] = jnp.zeros_like(mass)
    for h in range(2):
        rows = slice(h * 512, (h + 1) * 512)
        for n in range(2):
            cols = slice(n * 256, (n + 1) * 256)
            S[h, :, cols] = lax.dot_general(
                to[...], data[h * 512 + n * 256:h * 512 + (n + 1) * 256, :], NT, preferred_element_type=f32)
        m, l = softmax_pass(h, 512)
        stat2[h, 0, 0:1, :] = m
        stat2[h, 0, 1:2, :] = l
        for cp in stat_copies(stat2, h, 8, s2s, s2r, dppeer):
            cp.start()
    for h in range(2):
        wait_bytes(stat2.at[h, pl.ds(1, 7)], s2r.at[h])
        weights(h, combine(stat2, h, 8), h * 512, 512)
    msum[0] = jnp.sum(mass[...].T, axis=0, keepdims=True)
    m_copies = [pltpu.make_async_remote_copy(
        src_ref=msum.at[0], dst_ref=msum.at[r], send_sem=mss, recv_sem=msr,
        device_id=centpeer(r), device_id_type=MESH) for r in range(1, 16)]
    for cp in m_copies:
        cp.start()

    def moved_two(base, put):
        @pl.loop(0, 2)
        def _(t):
            src = pl.ds(pl.multiple_of(base + t * 256, 256), 256)
            dst = pl.ds(pl.multiple_of(t * 256, 256), 256)
            p = Pb[src, :]
            for d in range(3):
                cols = slice(d * 512, (d + 1) * 512)
                put(dst, cols, lax.dot_general(p, data[:, cols], NN, preferred_element_type=f32))

    def put_send(rows, cols, v):
        dsend[rows, cols] = v.astype(bf16)

    def put_own(rows, cols, v):
        acc[rows, cols] = v

    moved_two((1 - c) * 512, put_send)
    dcopy = pltpu.make_async_remote_copy(
        src_ref=dsend, dst_ref=drecv, send_sem=ds, recv_sem=dr, device_id=partner, device_id_type=MESH)
    dcopy.start()
    moved_two(c * 512, put_own)
    dcopy.wait_recv()
    blocks = []
    for r in (5, 4, 7, 6, 3, 2, 1):
        yy, zz = xor4(y, r // 2), flip(zl, r % 2)
        rows = pl.ds(pl.multiple_of(yy * 128 + zz * 64, 64), 64)
        snd[r] = (acc[rows, :] + drecv[rows, :].astype(f32)).astype(bf16)
        cp = pltpu.make_async_remote_copy(
            src_ref=snd.at[r], dst_ref=rcv.at[r], send_sem=rs.at[r], recv_sem=rr.at[r],
            device_id=dev(x, yy, zh, zz, c), device_id_type=MESH)
        cp.start()
        blocks.append(cp)
    rows = pl.ds(pl.multiple_of(y * 128 + zl * 64, 64), 64)
    trows = pl.ds(pl.multiple_of(c * 512 + y * 128 + zl * 64, 64), 64)
    wait_bytes(msum.at[pl.ds(1, 15)], msr)
    total = msum[0]
    for r in range(1, 16):
        total = total + msum[r]
    here = c * 512 + y * 128 + zl * 64
    lane = lax.broadcasted_iota(jnp.int32, (64, ROWS), 1)
    sub = lax.broadcasted_iota(jnp.int32, (64, ROWS), 0)
    col = jnp.sum(jnp.where(lane == sub + here, total, 0.0), axis=1, keepdims=True)
    own = acc[rows, :] + drecv[rows, :].astype(f32) + prior * to[trows, :].astype(f32)
    for cp in blocks:
        cp.wait_recv()
    for r in range(1, 8):
        own = own + rcv[r].astype(f32)
    snd[0] = (own * (1.0 / (col + prior))).astype(bf16)
    o2 = pltpu.make_async_copy(snd.at[0], out2.at[0], ld.at[1])
    o2.start()

    for cp in names.values():
        cp.wait_send()
    for j in range(8):
        wait_bytes(stat.at[j, pl.ds(1, 15)], ss.at[j])
    for h in range(2):
        wait_bytes(stat2.at[h, pl.ds(1, 7)], s2s.at[h])
    wait_bytes(msum.at[pl.ds(1, 15)], mss)
    dcopy.wait_send()
    for cp in blocks:
        cp.wait_send()
    o1.wait()
    o2.wait()


def body(images, cents, tops):
    anyspec = pl.BlockSpec(memory_space=pl.ANY)
    ncopies = 42
    flops = 2 * 2 * (1024 * 4096 + 1024 * 1024) * D
    return pl.pallas_call(
        kernel,
        out_shape=(jax.ShapeDtypeStruct((128, D), bf16), jax.ShapeDtypeStruct((1, 64, D), bf16)),
        in_specs=[anyspec] * 3,
        out_specs=(anyspec, anyspec),
        scratch_shapes=[
            pltpu.VMEM((2, 4, SHARD, D), bf16),
            pltpu.VMEM((ROWS, D), bf16),
            pltpu.VMEM((ROWS, D), bf16),
            pltpu.VMEM((2, ROWS, 512), f32),
            pltpu.VMEM((ROWS, 1024), bf16),
            pltpu.VMEM((ROWS, D), f32),
            pltpu.VMEM((ROWS, 128), f32),
            pltpu.VMEM((ROWS, D), bf16),
            pltpu.VMEM((8, 16, 2, 512), f32),
            pltpu.VMEM((2, 8, 2, 512), f32),
            pltpu.VMEM((16, 1, 1024), f32),
            pltpu.VMEM((512, D), bf16),
            pltpu.VMEM((512, D), bf16),
            pltpu.VMEM((8, 64, D), bf16),
            pltpu.VMEM((8, 64, D), bf16),
            pltpu.SemaphoreType.DMA((ncopies,)),
            pltpu.SemaphoreType.DMA((ncopies,)),
            pltpu.SemaphoreType.DMA((8,)),
            pltpu.SemaphoreType.DMA((8,)),
            pltpu.SemaphoreType.DMA((2,)),
            pltpu.SemaphoreType.DMA((2,)),
            pltpu.SemaphoreType.DMA,
            pltpu.SemaphoreType.DMA,
            pltpu.SemaphoreType.DMA,
            pltpu.SemaphoreType.DMA,
            pltpu.SemaphoreType.DMA((8,)),
            pltpu.SemaphoreType.DMA((8,)),
            pltpu.SemaphoreType.DMA((18,)),
        ],
        compiler_params=pltpu.CompilerParams(
            collective_id=0, has_side_effects=True, vmem_limit_bytes=60 * 1024 * 1024),
        cost_estimate=pl.CostEstimate(flops=flops, bytes_accessed=9 * 1024 * 1024, transcendentals=6 * 1024 * 1024),
        name="two_levels",
    )(images, cents, tops)


def solution(mesh):
    return jax.shard_map(
        body,
        mesh=mesh,
        in_specs=(P("dp", None), P("cent", None), P("dp", None)),
        out_specs=(P(("cent", "dp"), None), P("dp", "cent", None)),
        check_vma=False,
    )
```

```python
import jax
import jax.numpy as jnp
from jax import lax
from jax.experimental import pallas as pl
from jax.experimental.pallas import tpu as pltpu
from jax.sharding import PartitionSpec as P

prior = 0.1
MESH = pl.DeviceIdType.MESH
f32, bf16 = jnp.float32, jnp.bfloat16
NT = (((1,), (1,)), ((), ()))
NN = (((1,), (0,)), ((), ()))
D = 1536
SHARD = 512
ROWS = 1024
HX, HQ = 128, 32
KAPPA = D ** -0.5 * 1.4426950408889634
ORDER = (1, 3, 2)
AT_X = {(0, 1): 1024, (0, 3): 1152, (0, 2): 2048, (1, 1): 2560, (1, 3): 3072, (1, 2): 3584}
AT_Y = {(0, 1): 1536, (0, 3): 1792, (0, 2): 2304, (1, 1): 2816, (1, 3): 3328, (1, 2): 3840}
CHUNKS = (0, 1024, 1536, 512, 2048, 2560, 3072, 3584)
SLOTS = 4
FIRST = (
    ('xx', 1, 0), ('xx', 3, 0), ('xq', 0, 1), ('xq', 0, 3), ('zr', 0), ('zq',), ('zr', 1), ('zr', 2),
    ('zr', 3), ('xx', 1, 1), ('xx', 3, 1), ('xq', 0, 2),
)
SECOND = (
    ('xq', 1, 1), ('xq', 1, 3), ('xq', 1, 2), ('dzq',),
)
STEPS = (
    ('B', 0, 0), ('xr', 1, 0), ('xr', 3, 0), ('zrs', 0), ('B', 0, 1), ('zqs',), ('yf', 0, 1), ('yf', 0, 3),
    ('zrs', 1), ('A', 1, 0), ('zrs', 2), ('zrs', 3), ('yr', 0, 1, 1), ('yr', 0, 1, 3), ('xr', 1, 1),
    ('xr', 3, 1), ('zis', 0), ('zis', 1), ('yr', 0, 3, 1), ('yr', 0, 3, 3), ('zis', 2), ('yf', 0, 2),
    ('yr', 0, 1, 2), ('A', 1, 1), ('zis', 3), ('A', 1, 2), ('yf', 1, 1), ('yr', 0, 3, 2), ('A', 2, 0),
    ('l', 1), ('xr', 2, 0), ('yr', 0, 2, 3), ('yr', 0, 2, 1), ('A', 2, 1), ('A', 2, 2), ('A', 3, 0),
    ('yf', 1, 3), ('A', 3, 1), ('l', 3), ('yr', 0, 2, 2), ('yr', 1, 1, 1), ('yr', 1, 1, 3), ('A', 3, 2),
    ('xr', 2, 1), ('B', 1, 0), ('yf', 1, 2), ('B', 1, 1), ('lis', 1), ('yr', 1, 3, 3), ('yr', 1, 3, 1),
    ('A', 4, 0), ('yr', 1, 1, 2), ('A', 4, 1), ('A', 4, 2), ('A', 5, 0), ('l', 2), ('lis', 3),
    ('yr', 1, 2, 1), ('yr', 1, 2, 3), ('A', 5, 1), ('yr', 1, 3, 2), ('A', 5, 2), ('B', 2, 0), ('B', 2, 1),
    ('yr', 1, 2, 2), ('A', 6, 0), ('A', 6, 1), ('lis', 2), ('A', 6, 2), ('B', 3, 0), ('B', 3, 1), ('A', 7, 0),
    ('A', 7, 1), ('A', 7, 2), ('B', 4, 0), ('B', 4, 1), ('B', 5, 0), ('B', 5, 1), ('B', 6, 0), ('B', 6, 1),
    ('B', 7, 0), ('B', 7, 1),
)


def xor4(v, r):
    if r == 0:
        return v
    if r == 1:
        return v + 1 - 2 * lax.rem(v, 2)
    if r == 2:
        return lax.rem(v + 2, 4)
    return 3 - v


def flip(v, r):
    return 1 - v if r else v


def kernel(images, cents, tops, out1, out2,
           img, ce, to, S, Pb, acc, mass, data, stat, stat2, msum, dsend, drecv, zs, zr, ys, yr, y2s, y2r, z2s, z2r, res,
           gs, gr, ss, sr, s2s, s2r, mss, msr, ds, dr, rs, rr, ld):
    ci = lax.axis_index("cent")
    di = lax.axis_index("dp")
    y, zl, c = lax.div(ci, 4), lax.rem(lax.div(ci, 2), 2), lax.rem(ci, 2)
    x, zh = lax.div(di, 2), lax.rem(di, 2)

    def dev(x, y, zh, zl, c):
        return ((y * 2 + zl) * 2 + c, x * 2 + zh)

    def centpeer(r):
        return dev(x, xor4(y, r // 4), zh, flip(zl, (r // 2) % 2), flip(c, r % 2))

    def dppeer(r):
        return dev(xor4(x, r // 2), y, flip(zh, r % 2), zl, c)

    partner = centpeer(1)
    zpeer = dev(x, y, 1 - zh, 1 - zl, c)

    l_img = pltpu.make_async_copy(images, img.at[pl.ds(0, SHARD)], ld.at[0])
    l_ce = pltpu.make_async_copy(cents, ce, ld.at[1])
    l_img.start()
    l_ce.start()
    l_to = []
    for b in range(16):
        yy, zz, cc = b // 4, (b // 2) % 2, b % 2
        pos = cc * 512 + yy * 128 + zz * 64
        l_to.append(pltpu.make_async_copy(tops.at[pl.ds(b * 64, 64)], to.at[pl.ds(pos, 64)], ld.at[2 + b]))

    barrier = pltpu.get_barrier_semaphore()
    everyone = [centpeer(r) for r in range(1, 16)] + [dppeer(r) for r in range(1, 8)] + [zpeer]
    for p in everyone:
        pl.semaphore_signal(barrier, inc=1, device_id=p, device_id_type=MESH)

    names = {}

    def copy(name, src, dst, device):
        i = len(names)
        names[name] = pltpu.make_async_remote_copy(
            src_ref=src, dst_ref=dst, send_sem=gs.at[i], recv_sem=gr.at[i],
            device_id=device, device_id_type=MESH)

    def rq(at, q, core):
        return pl.ds(pl.multiple_of(at + q * 64 + core * HQ, 16), HQ)

    def rqh(at, q, core, h):
        return pl.ds(pl.multiple_of(at + q * 64 + core * HQ + h * 16, 16), 16)

    def rxh(at, core, h):
        return pl.ds(pl.multiple_of(at + core * HX + h * 64, 16), 64)

    def near(s, core, h):
        if s == 2:
            return rxh(AT_X[0, 2], core, h)
        return pl.ds(pl.multiple_of(AT_X[0, s] + h * 256 + core * 64, 16), 64)

    zinner = centpeer(2)
    rows = rq(256, y, c)
    rows1 = rq(768, y, c)
    copy(("zq",), img.at[rows], img.at[rows1], zpeer)
    copy(("dzq",), img.at[rows1], img.at[rows1], partner)
    for k in range(4):
        def part(at, h):
            return rxh(at, c, h) if k == 0 else rqh(at + 256, xor4(y, k), c, h)
        copy(("zr", k), img.at[part(0, 1 - zl)], img.at[part(512, 1 - zl)], zpeer)
        copy(("zi", k), img.at[part(512, zl)], img.at[part(512, zl)], zinner)
        copy(("dzr", k), img.at[part(512, zl)], img.at[part(512, zl)], partner)
        copy(("dzi", k), img.at[part(512, 1 - zl)], img.at[part(512, 1 - zl)], partner)
    for s in ORDER:
        device = dev(xor4(x, s), y, zh, zl, c)
        for h in range(2):
            if s != 2:
                copy(("xx", s, h), img.at[rxh(0, c, h)], img.at[near(s, c, h)], device)
            copy(("dxx", s, h), img.at[near(s, c, h)], img.at[near(s, c, h)], partner)
        if s != 2:
            h = 0 if s == 1 else 1
            copy(("xf", s), img.at[near(s, c, h)], img.at[near(2, c, h)], dev(xor4(x, 4 - s), y, zh, zl, c))
        b = AT_X[1, s]
        copy(("lr", s), img.at[near(s, c, 1 - zl)], img.at[rxh(b, c, 1 - zl)], zpeer)
        copy(("li", s), img.at[rxh(b, c, zl)], img.at[rxh(b, c, zl)], zinner)
        copy(("dlr", s), img.at[rxh(b, c, zl)], img.at[rxh(b, c, zl)], partner)
        copy(("dli", s), img.at[rxh(b, c, 1 - zl)], img.at[rxh(b, c, 1 - zl)], partner)
        for z in range(2):
            rows = rq(AT_Y[z, s], y, c)
            copy(("xq", z, s), img.at[rq(z * SHARD + 256, y, c)], img.at[rows], device)
            for r in (1, 3):
                copy(("yq", z, s, r), img.at[rows], img.at[rows], dev(x, xor4(y, r), zh, zl, c))
                there = rqh(AT_Y[z, s], xor4(y, r), c, 0 if r == 1 else 1)
                copy(("yh", z, s, r), img.at[there], img.at[there], dev(x, xor4(y, 4 - r), zh, zl, c))
            for r in range(4):
                there = rq(AT_Y[z, s], xor4(y, r), c)
                copy(("dq", z, s, r), img.at[there], img.at[there], partner)

    def start(*ns):
        for n in ns:
            names[n].start()

    here_now = set()

    def arrive(*ns):
        for n in ns:
            if n not in here_now:
                here_now.add(n)
                names[n].wait_recv()

    relay = {("zqs",): ([("zq",)], SECOND)}
    for k in range(4):
        relay["zrs", k] = ([("zr", k)], [("zi", k), ("dzr", k)])
        relay["zis", k] = ([("zi", k)], [("dzi", k)])
    for s in ORDER:
        relay["l", s] = ([("lr", s)], [("li", s), ("dlr", s)])
        relay["lis", s] = ([("li", s)], [("dli", s)])
        if s == 2:
            relay["xr", 2, 0] = ([("xf", 1)], [("dxx", 2, 0)])
            relay["xr", 2, 1] = ([("xf", 1), ("xf", 3)], [("lr", 2), ("dxx", 2, 1)])
        else:
            relay["xr", s, 0] = ([("xx", s, 0)], ([("xf", s)] if s == 1 else []) + [("dxx", s, 0)])
            relay["xr", s, 1] = ([("xx", s, 0), ("xx", s, 1)],
                                 ([("xf", s)] if s == 3 else []) + [("lr", s), ("dxx", s, 1)])
        for z in range(2):
            relay["yf", z, s] = ([("xq", z, s)], [("yq", z, s, 1), ("yq", z, s, 3), ("dq", z, s, 0)])
            for r in (1, 3):
                relay["yr", z, s, r] = ([("yq", z, s, r)], [("yh", z, s, r), ("dq", z, s, r)])
            relay["yr", z, s, 2] = ([("yh", z, s, 1), ("yh", z, s, 3)], [("dq", z, s, 2)])

    def ready(at):
        if at == 512:
            arrive(("dzr", 0), ("dzi", 0))
        if at == 768:
            arrive(("dzq",), *[(n, k) for n in ("dzr", "dzi") for k in range(1, 4)])
        if at in (1024, 1280):
            h = (at - 1024) // 256
            arrive(("dxx", 1, h), ("dxx", 3, h))
        elif at == AT_X[0, 2]:
            arrive(("dxx", 2, 0), ("dxx", 2, 1))
        for (z, s), a in AT_X.items():
            if z and at == a:
                arrive(("dlr", s), ("dli", s))
        for key, a in AT_Y.items():
            if at == a:
                arrive(*[("dq",) + key + (r,) for r in range(4)])

    l_img.wait()
    l_ce.wait()

    mass[...] = jnp.zeros_like(mass)

    def soft(sl):
        ms, ls = [], []
        for n in (slice(0, 256), slice(256, 512)):
            m = jnp.max(S[sl, :, n], axis=0, keepdims=True)
            l = jnp.zeros((8, 256), f32)
            for t in range(0, ROWS, 128):
                e = jnp.exp2((S[sl, t:t + 128, n] - m) * KAPPA)
                S[sl, t:t + 128, n] = e
                l = l + jnp.sum(e.reshape(16, 8, 256), axis=0)
            ms.append(m)
            ls.append(jnp.sum(l, axis=0, keepdims=True))
        return jnp.concatenate(ms, axis=1), jnp.concatenate(ls, axis=1)

    def stat_copies(buf, j, count, ssem, rsem, peer):
        return [pltpu.make_async_remote_copy(
            src_ref=buf.at[j, 0], dst_ref=buf.at[j, r], send_sem=ssem.at[j], recv_sem=rsem.at[j],
            device_id=peer(r), device_id_type=MESH) for r in range(1, count)]

    def scores(sl, left, right, lo):
        for n in range(2):
            cols = slice(n * 256, (n + 1) * 256)
            S[sl, :, cols] = lax.dot_general(
                left[...], right[lo + n * 256:lo + (n + 1) * 256, :], NT, preferred_element_type=f32)
        return soft(sl)

    def combine(buf, j, count):
        ms = [buf[j, r, 0:1, :] for r in range(count)]
        M = ms[0]
        for v in ms[1:]:
            M = jnp.maximum(M, v)
        L = jnp.zeros_like(M)
        for r in range(count):
            L = L + buf[j, r, 1:2, :] * jnp.exp2((ms[r] - M) * KAPPA)
        return jnp.exp2((ms[0] - M) * KAPPA) / L

    def wait_bytes(ref, sem):
        pltpu.make_async_copy(ref, ref, sem).wait()

    def weights(sl, f, rows):
        p = S[sl, rows, :] * f
        q = p[:, 0:128]
        for i in range(1, 4):
            q = q + p[:, i * 128:(i + 1) * 128]
        mass[rows, :] += q
        return p.astype(bf16)

    def A(j, part):
        at, sl = CHUNKS[j] + 256 * part, j % SLOTS
        if part < 2:
            ready(at)
            S[sl, :, part * 256:(part + 1) * 256] = lax.dot_general(
                ce[...], img[at:at + 256, :], NT, preferred_element_type=f32)
        else:
            m, l = soft(sl)
            stat[j, 0, 0:1, :] = m
            stat[j, 0, 1:2, :] = l
            if j:
                send_stats(j)

    def send_stats(j):
        for cp in stat_copies(stat, j, 16, ss, sr, centpeer):
            cp.start()

    factors = {}

    def B(j, part):
        at = CHUNKS[j]
        if part == 0:
            wait_bytes(stat.at[j, pl.ds(1, 15)], sr.at[j])
            factors[j] = combine(stat, j, 16)
        rows = slice(part * 512, (part + 1) * 512)
        p = weights(j % SLOTS, factors[j], rows)
        for d in range(3):
            cols = slice(d * 512, (d + 1) * 512)
            v = lax.dot_general(p, img[at:at + 512, cols], NN, preferred_element_type=f32)
            if j == 0:
                acc[rows, cols] = v
            else:
                acc[rows, cols] += v

    for part in range(3):
        A(0, part)
    pl.semaphore_wait(barrier, len(everyone))
    start(*FIRST)
    send_stats(0)
    for l in l_to:
        l.start()
    for step in STEPS:
        if step[0] == "A":
            A(*step[1:])
        elif step[0] == "B":
            B(*step[1:])
        else:
            arrive(*relay[step][0])
            start(*relay[step][1])

    for t in range(0, ROWS, 256):
        rows = slice(t, t + 256)
        inv = 1.0 / (jnp.sum(mass[rows, :], axis=1, keepdims=True) + prior)
        data[rows, :] = ((acc[rows, :] + prior * ce[rows, :].astype(f32)) * inv).astype(bf16)
    o1 = pltpu.make_async_copy(data.at[pl.ds(pl.multiple_of(di * 128, 128), 128)], out1, ld.at[0])
    o1.start()

    for l in l_to:
        l.wait()
    mass[...] = jnp.zeros_like(mass)
    for h in range(2):
        m, l = scores(h, to, data, h * 512)
        stat2[h, 0, 0:1, :] = m
        stat2[h, 0, 1:2, :] = l
        for cp in stat_copies(stat2, h, 8, s2s, s2r, dppeer):
            cp.start()
    wait_bytes(stat2.at[0, pl.ds(1, 7)], s2r.at[0])
    f = combine(stat2, 0, 8)
    for t in range(0, ROWS, 512):
        rows = slice(t, t + 512)
        p = weights(0, f, rows)
        for d in range(3):
            cols = slice(d * 512, (d + 1) * 512)
            acc[rows, cols] = lax.dot_general(p, data[0:512, cols], NN, preferred_element_type=f32)
    wait_bytes(stat2.at[1, pl.ds(1, 7)], s2r.at[1])
    f = combine(stat2, 1, 8)
    for t in range(0, ROWS, 512):
        rows = slice(t, t + 512)
        Pb[rows, :] = weights(1, f, rows)
    msum[0] = jnp.sum(mass[...].T, axis=0, keepdims=True)
    m_copies = [pltpu.make_async_remote_copy(
        src_ref=msum.at[0], dst_ref=msum.at[r], send_sem=mss, recv_sem=msr,
        device_id=centpeer(r), device_id_type=MESH) for r in range(1, 16)]
    for cp in m_copies:
        cp.start()

    pair = lax.div(y, 2)
    d_copies = []
    for i in range(2):
        half = pl.multiple_of((1 - pair if i == 0 else pair) * 256, 256)
        src = pl.ds(pl.multiple_of((1 - c) * 512 + half, 256), 256)
        for d in range(3):
            cols = slice(d * 512, (d + 1) * 512)
            v = acc[src, cols] + lax.dot_general(Pb[src, :], data[512:1024, cols], NN, preferred_element_type=f32)
            dsend[pl.ds(half, 256), cols] = v.astype(bf16)
        cp = pltpu.make_async_remote_copy(
            src_ref=dsend.at[pl.ds(half, 256)], dst_ref=drecv.at[pl.ds(half, 256)],
            send_sem=ds.at[i], recv_sem=dr.at[i], device_id=partner, device_id_type=MESH)
        cp.start()
        d_copies.append(cp)
    blocks = []

    def send(i, src, dst, device):
        cp = pltpu.make_async_remote_copy(
            src_ref=src, dst_ref=dst, send_sem=rs.at[i], recv_sem=rr.at[i], device_id=device, device_id_type=MESH)
        cp.start()
        blocks.append(cp)
        return cp

    def at(yy, zz):
        return pl.ds(pl.multiple_of(c * 512 + yy * 128 + zz * 64, 64), 64)

    zpartner = dev(x, y, zh, 1 - zl, c)
    LEFT, RIGHT = slice(0, D // 2), slice(D // 2, D)
    along_y, along_z = {}, {}
    for i in range(2):
        half = pl.multiple_of((1 - pair if i == 0 else pair) * 256, 256)
        src = pl.ds(pl.multiple_of(c * 512 + half, 256), 256)
        for d in range(3):
            cols = slice(d * 512, (d + 1) * 512)
            acc[src, cols] += lax.dot_general(Pb[src, :], data[512:1024, cols], NN, preferred_element_type=f32)
        d_copies[i].wait_recv()
        acc[src, :] += drecv[pl.ds(half, 256), :].astype(f32)
        for r in ((2, 3) if i == 0 else (1, 0)):
            yy = xor4(y, r)
            zs[r] = acc[at(yy, 1 - zl), RIGHT].astype(bf16)
            along_z[r] = send(r, zs.at[r], zr.at[r], zpartner)
            if r:
                rows = pl.ds(pl.multiple_of(c * 512 + yy * 128, 128), 128)
                ys[r] = acc[rows, LEFT].astype(bf16)
                along_y[r] = send(4 + r, ys.at[r], yr.at[r], dev(x, yy, zh, zl, c))
    along_y2 = {}
    for r in (2, 3, 1):
        yy = xor4(y, r)
        along_z[r].wait_recv()
        y2s[r] = (acc[at(yy, zl), RIGHT] + zr[r].astype(f32)).astype(bf16)
        along_y2[r] = send(8 + r, y2s.at[r], y2r.at[r], dev(x, yy, zh, zl, c))
    here = c * 512 + y * 128 + zl * 64
    wait_bytes(msum.at[pl.ds(1, 15)], msr)
    total = msum[0]
    for r in range(1, 16):
        total = total + msum[r]
    lane = lax.broadcasted_iota(jnp.int32, (64, ROWS), 1)
    sub = lax.broadcasted_iota(jnp.int32, (64, ROWS), 0)
    col = jnp.sum(jnp.where(lane == sub + here, total, 0.0), axis=1, keepdims=True)
    inv = 1.0 / (col + prior)
    for r in (2, 3, 1):
        along_y[r].wait_recv()

    def left(zz):
        rows = pl.ds(pl.multiple_of(zz * 64, 64), 64)
        v = acc[at(y, zz), LEFT]
        for r in (1, 2, 3):
            v = v + yr[r, rows, :].astype(f32)
        return v

    z2s[...] = left(1 - zl).astype(bf16)
    along_z2 = send(12, z2s, z2r, zpartner)
    own = left(zl) + prior * to[at(y, zl), LEFT].astype(f32)
    along_z[0].wait_recv()
    right = acc[at(y, zl), RIGHT] + prior * to[at(y, zl), RIGHT].astype(f32) + zr[0].astype(f32)
    for r in (2, 3, 1):
        along_y2[r].wait_recv()
        right = right + y2r[r].astype(f32)
    res[:, RIGHT] = (right * inv).astype(bf16)
    along_z2.wait_recv()
    res[:, LEFT] = ((own + z2r[...].astype(f32)) * inv).astype(bf16)
    o2 = pltpu.make_async_copy(res, out2, ld.at[1])
    o2.start()

    for cp in names.values():
        cp.wait_send()
    for j in range(8):
        wait_bytes(stat.at[j, pl.ds(1, 15)], ss.at[j])
    for h in range(2):
        wait_bytes(stat2.at[h, pl.ds(1, 7)], s2s.at[h])
    wait_bytes(msum.at[pl.ds(1, 15)], mss)
    for cp in d_copies + blocks:
        cp.wait_send()
    o1.wait()
    o2.wait()


def hand_over(a, b, out1, out2):
    out1[...] = a[...]
    out2[0] = b[...]


def body(images, cents, tops):
    anyspec = pl.BlockSpec(memory_space=pl.ANY)
    vmem = pl.BlockSpec(memory_space=pltpu.VMEM)
    ncopies = 96
    flops = 2 * 2 * (1024 * 4096 + 1024 * 1024) * D
    part, top = pl.pallas_call(
        kernel,
        out_shape=(jax.ShapeDtypeStruct((128, D), bf16), jax.ShapeDtypeStruct((64, D), bf16)),
        in_specs=[anyspec] * 3,
        out_specs=(anyspec, anyspec),
        scratch_shapes=[
            pltpu.VMEM((8 * SHARD, D), bf16),
            pltpu.VMEM((ROWS, D), bf16),
            pltpu.VMEM((ROWS, D), bf16),
            pltpu.VMEM((SLOTS, ROWS, 512), f32),
            pltpu.VMEM((ROWS, 512), bf16),
            pltpu.VMEM((ROWS, D), f32),
            pltpu.VMEM((ROWS, 128), f32),
            pltpu.VMEM((ROWS, D), bf16),
            pltpu.VMEM((8, 16, 2, 512), f32),
            pltpu.VMEM((2, 8, 2, 512), f32),
            pltpu.VMEM((16, 1, 1024), f32),
            pltpu.VMEM((512, D), bf16),
            pltpu.VMEM((512, D), bf16),
            pltpu.VMEM((4, 64, D // 2), bf16),
            pltpu.VMEM((4, 64, D // 2), bf16),
            pltpu.VMEM((4, 128, D // 2), bf16),
            pltpu.VMEM((4, 128, D // 2), bf16),
            pltpu.VMEM((4, 64, D // 2), bf16),
            pltpu.VMEM((4, 64, D // 2), bf16),
            pltpu.VMEM((64, D // 2), bf16),
            pltpu.VMEM((64, D // 2), bf16),
            pltpu.VMEM((64, D), bf16),
            pltpu.SemaphoreType.DMA((ncopies,)),
            pltpu.SemaphoreType.DMA((ncopies,)),
            pltpu.SemaphoreType.DMA((8,)),
            pltpu.SemaphoreType.DMA((8,)),
            pltpu.SemaphoreType.DMA((2,)),
            pltpu.SemaphoreType.DMA((2,)),
            pltpu.SemaphoreType.DMA,
            pltpu.SemaphoreType.DMA,
            pltpu.SemaphoreType.DMA((2,)),
            pltpu.SemaphoreType.DMA((2,)),
            pltpu.SemaphoreType.DMA((13,)),
            pltpu.SemaphoreType.DMA((13,)),
            pltpu.SemaphoreType.DMA((18,)),
        ],
        compiler_params=pltpu.CompilerParams(
            collective_id=0, has_side_effects=True, vmem_limit_bytes=60 * 1024 * 1024),
        cost_estimate=pl.CostEstimate(flops=flops, bytes_accessed=9 * 1024 * 1024, transcendentals=6 * 1024 * 1024),
        name="two_levels",
    )(images, cents, tops)
    return pl.pallas_call(
        hand_over,
        out_shape=(jax.ShapeDtypeStruct((128, D), bf16), jax.ShapeDtypeStruct((1, 64, D), bf16)),
        in_specs=[vmem] * 2,
        out_specs=(vmem, vmem),
        name="hand_over",
    )(part, top)


def solution(mesh):
    return jax.shard_map(
        body,
        mesh=mesh,
        in_specs=(P("dp", None), P("cent", None), P("dp", None)),
        out_specs=(P(("cent", "dp"), None), P("dp", "cent", None)),
        check_vma=False,
    )
```

```python
import jax
import jax.numpy as jnp
from jax import lax
from jax.experimental import pallas as pl
from jax.experimental.pallas import tpu as pltpu
from jax.sharding import PartitionSpec as P

prior = 0.1
MESH = pl.DeviceIdType.MESH
f32, bf16 = jnp.float32, jnp.bfloat16
NT = (((1,), (1,)), ((), ()))
NN = (((1,), (0,)), ((), ()))
D = 1536
SHARD = 512
ROWS = 1024
HX, HQ = 128, 32
KAPPA = D ** -0.5 * 1.4426950408889634
ORDER = (1, 3, 2)
AT_X = {(0, 1): 1024, (0, 3): 1152, (0, 2): 2048, (1, 1): 2560, (1, 3): 3072, (1, 2): 3584}
AT_Y = {(0, 1): 1536, (0, 3): 1792, (0, 2): 2304, (1, 1): 2816, (1, 3): 3328, (1, 2): 3840}
CHUNKS = (0, 1024, 512, 1536, 2048, 2560, 3072, 3584)
SLOTS = 4
FIRST = (
    ('xx', 1, 0), ('xx', 3, 0), ('xq', 0, 1), ('xq', 0, 3), ('zr', 0), ('zq',), ('zr', 1), ('zr', 2),
    ('zr', 3), ('xx', 1, 1), ('xx', 3, 1), ('xq', 0, 2),
)
SECOND = (
    ('xq', 1, 1), ('xq', 1, 3), ('xq', 1, 2), ('dzq',),
)
STEPS = (
    ('B', 0), ('xr', 1, 0), ('xr', 3, 0), ('zrs', 0), ('zqs',), ('yf', 0, 1), ('yf', 0, 3), ('zrs', 1),
    ('zrs', 2), ('zrs', 3), ('yr', 0, 1, 1), ('yr', 0, 1, 3), ('xr', 1, 1), ('xr', 3, 1), ('zis', 0),
    ('yr', 0, 3, 1), ('yr', 0, 3, 3), ('zis', 1), ('yf', 0, 2), ('yr', 0, 1, 2), ('A', 1), ('yf', 1, 1),
    ('l', 1, 0), ('zis', 2), ('zis', 3), ('yr', 0, 3, 2), ('l', 1, 1), ('xr', 2, 0), ('yr', 0, 2, 3),
    ('yr', 0, 2, 1), ('A', 2), ('yf', 1, 3), ('l', 3, 0), ('l', 3, 1), ('lis', 1, 0), ('yr', 1, 1, 1),
    ('yr', 1, 1, 3), ('A', 3), ('yf', 1, 2), ('xr', 2, 1), ('lis', 1, 1), ('yr', 0, 2, 2), ('B', 1),
    ('lis', 3, 0), ('yr', 1, 3, 1), ('yr', 1, 3, 3), ('A', 4), ('l', 2, 0), ('lis', 3, 1), ('yr', 1, 1, 2),
    ('B', 2), ('l', 2, 1), ('yr', 1, 3, 2), ('yr', 1, 2, 1), ('yr', 1, 2, 3), ('B', 3), ('lis', 2, 0),
    ('A', 5), ('lis', 2, 1), ('yr', 1, 2, 2), ('A', 6), ('A', 7), ('B', 4), ('B', 5), ('B', 6), ('B', 7),
)


def xor4(v, r):
    if r == 0:
        return v
    if r == 1:
        return v + 1 - 2 * lax.rem(v, 2)
    if r == 2:
        return lax.rem(v + 2, 4)
    return 3 - v


def flip(v, r):
    return 1 - v if r else v


def kernel(images, cents, tops, out1, out2,
           img, ce, to, S, Pb, acc, mass, data, stat, stat2, msum, dsend, drecv, zs, zr, fs, fr, ys, yr, y2s, y2r, z2s, z2r, res,
           gs, gr, ss, sr, s2s, s2r, mss, msr, ds, dr, rs, rr, ld):
    ci = lax.axis_index("cent")
    di = lax.axis_index("dp")
    y, zl, c = lax.div(ci, 4), lax.rem(lax.div(ci, 2), 2), lax.rem(ci, 2)
    x, zh = lax.div(di, 2), lax.rem(di, 2)

    def dev(x, y, zh, zl, c):
        return ((y * 2 + zl) * 2 + c, x * 2 + zh)

    def centpeer(r):
        return dev(x, xor4(y, r // 4), zh, flip(zl, (r // 2) % 2), flip(c, r % 2))

    def dppeer(r):
        return dev(xor4(x, r // 2), y, flip(zh, r % 2), zl, c)

    partner = centpeer(1)
    zpeer = dev(x, y, 1 - zh, 1 - zl, c)

    l_img = pltpu.make_async_copy(images, img.at[pl.ds(0, SHARD)], ld.at[0])
    l_ce = pltpu.make_async_copy(cents, ce, ld.at[1])
    l_img.start()
    l_ce.start()
    l_to = []
    for b in range(16):
        yy, zz, cc = b // 4, (b // 2) % 2, b % 2
        pos = cc * 512 + yy * 128 + zz * 64
        l_to.append(pltpu.make_async_copy(tops.at[pl.ds(b * 64, 64)], to.at[pl.ds(pos, 64)], ld.at[2 + b]))

    barrier = pltpu.get_barrier_semaphore()
    everyone = [centpeer(r) for r in range(1, 16)] + [dppeer(r) for r in range(1, 8)] + [zpeer]
    for p in everyone:
        pl.semaphore_signal(barrier, inc=1, device_id=p, device_id_type=MESH)

    names = {}

    def copy(name, src, dst, device):
        i = len(names)
        names[name] = pltpu.make_async_remote_copy(
            src_ref=src, dst_ref=dst, send_sem=gs.at[i], recv_sem=gr.at[i],
            device_id=device, device_id_type=MESH)

    def rq(at, q, core):
        return pl.ds(pl.multiple_of(at + q * 64 + core * HQ, 16), HQ)

    def rqh(at, q, core, h):
        return pl.ds(pl.multiple_of(at + q * 64 + core * HQ + h * 16, 16), 16)

    def rxh(at, core, h):
        return pl.ds(pl.multiple_of(at + core * HX + h * 64, 16), 64)

    def near_at(s, core, h):
        if s == 2:
            return AT_X[0, 2] + core * HX + h * 64
        return AT_X[0, s] + h * 256 + core * 64

    def near(s, core, h):
        return pl.ds(pl.multiple_of(near_at(s, core, h), 16), 64)

    zinner = centpeer(2)
    rows = rq(256, y, c)
    rows1 = rq(768, y, c)
    copy(("zq",), img.at[rows], img.at[rows1], zpeer)
    copy(("dzq",), img.at[rows1], img.at[rows1], partner)
    for k in range(4):
        def part(at, h):
            return rxh(at, c, h) if k == 0 else rqh(at + 256, xor4(y, k), c, h)
        copy(("zr", k), img.at[part(0, 1 - zl)], img.at[part(512, 1 - zl)], zpeer)
        copy(("zi", k), img.at[part(512, zl)], img.at[part(512, zl)], zinner)
        copy(("dzr", k), img.at[part(512, zl)], img.at[part(512, zl)], partner)
        copy(("dzi", k), img.at[part(512, 1 - zl)], img.at[part(512, 1 - zl)], partner)
    for s in ORDER:
        device = dev(xor4(x, s), y, zh, zl, c)
        for h in range(2):
            if s != 2:
                copy(("xx", s, h), img.at[rxh(0, c, h)], img.at[near(s, c, h)], device)
            copy(("dxx", s, h), img.at[near(s, c, h)], img.at[near(s, c, h)], partner)
        if s != 2:
            h = 0 if s == 1 else 1
            copy(("xf", s), img.at[near(s, c, h)], img.at[near(2, c, h)], dev(xor4(x, 4 - s), y, zh, zl, c))
        for g in range(2):
            def there(core, h):
                return pl.ds(pl.multiple_of(AT_X[1, s] + core * HX + h * 64 + g * 32, 16), 32)
            src = pl.ds(pl.multiple_of(near_at(s, c, 1 - zl) + g * 32, 16), 32)
            copy(("lr", s, g), img.at[src], img.at[there(c, 1 - zl)], zpeer)
            copy(("li", s, g), img.at[there(c, zl)], img.at[there(c, zl)], zinner)
            copy(("dlr", s, g), img.at[there(c, zl)], img.at[there(c, zl)], partner)
            copy(("dli", s, g), img.at[there(c, 1 - zl)], img.at[there(c, 1 - zl)], partner)
        for z in range(2):
            rows = rq(AT_Y[z, s], y, c)
            copy(("xq", z, s), img.at[rq(z * SHARD + 256, y, c)], img.at[rows], device)
            for r in (1, 3):
                copy(("yq", z, s, r), img.at[rows], img.at[rows], dev(x, xor4(y, r), zh, zl, c))
                there = rqh(AT_Y[z, s], xor4(y, r), c, 0 if r == 1 else 1)
                copy(("yh", z, s, r), img.at[there], img.at[there], dev(x, xor4(y, 4 - r), zh, zl, c))
            for r in range(4):
                there = rq(AT_Y[z, s], xor4(y, r), c)
                copy(("dq", z, s, r), img.at[there], img.at[there], partner)

    def start(*ns):
        for n in ns:
            names[n].start()

    here_now = set()

    def arrive(*ns):
        for n in ns:
            if n not in here_now:
                here_now.add(n)
                names[n].wait_recv()

    relay = {("zqs",): ([("zq",)], SECOND)}
    for k in range(4):
        relay["zrs", k] = ([("zr", k)], [("zi", k), ("dzr", k)])
        relay["zis", k] = ([("zi", k)], [("dzi", k)])
    for s in ORDER:
        for g in range(2):
            relay["l", s, g] = ([("lr", s, g)], [("li", s, g), ("dlr", s, g)])
            relay["lis", s, g] = ([("li", s, g)], [("dli", s, g)])
        if s == 2:
            relay["xr", 2, 0] = ([("xf", 1)], [("dxx", 2, 0)])
            relay["xr", 2, 1] = ([("xf", 1), ("xf", 3)], [("lr", 2, 0), ("lr", 2, 1), ("dxx", 2, 1)])
        else:
            relay["xr", s, 0] = ([("xx", s, 0)], ([("xf", s)] if s == 1 else []) + [("dxx", s, 0)])
            relay["xr", s, 1] = ([("xx", s, 0), ("xx", s, 1)],
                                 ([("xf", s)] if s == 3 else []) + [("lr", s, 0), ("lr", s, 1), ("dxx", s, 1)])
        for z in range(2):
            relay["yf", z, s] = ([("xq", z, s)], [("yq", z, s, 1), ("yq", z, s, 3), ("dq", z, s, 0)])
            for r in (1, 3):
                relay["yr", z, s, r] = ([("yq", z, s, r)], [("yh", z, s, r), ("dq", z, s, r)])
            relay["yr", z, s, 2] = ([("yh", z, s, 1), ("yh", z, s, 3)], [("dq", z, s, 2)])

    def ready(at):
        if at == 512:
            arrive(("dzr", 0), ("dzi", 0))
        if at == 768:
            arrive(("dzq",), *[(n, k) for n in ("dzr", "dzi") for k in range(1, 4)])
        if at in (1024, 1280):
            h = (at - 1024) // 256
            arrive(("dxx", 1, h), ("dxx", 3, h))
        elif at == AT_X[0, 2]:
            arrive(("dxx", 2, 0), ("dxx", 2, 1))
        for (z, s), a in AT_X.items():
            if z and at == a:
                arrive(*[(n, s, g) for n in ("dlr", "dli") for g in range(2)])
        for key, a in AT_Y.items():
            if at == a:
                arrive(*[("dq",) + key + (r,) for r in range(4)])

    l_img.wait()
    l_ce.wait()

    mass[...] = jnp.zeros_like(mass)

    def soft(sl):
        ms, ls = [], []
        for n in (slice(0, 256), slice(256, 512)):
            m = jnp.max(S[sl, :, n], axis=0, keepdims=True)
            l = jnp.zeros((8, 256), f32)
            for t in range(0, ROWS, 128):
                e = jnp.exp2((S[sl, t:t + 128, n] - m) * KAPPA)
                S[sl, t:t + 128, n] = e
                l = l + jnp.sum(e.reshape(16, 8, 256), axis=0)
            ms.append(m)
            ls.append(jnp.sum(l, axis=0, keepdims=True))
        return jnp.concatenate(ms, axis=1), jnp.concatenate(ls, axis=1)

    def stat_copies(buf, j, count, ssem, rsem, peer):
        return [pltpu.make_async_remote_copy(
            src_ref=buf.at[j, 0], dst_ref=buf.at[j, r], send_sem=ssem.at[j], recv_sem=rsem.at[j],
            device_id=peer(r), device_id_type=MESH) for r in range(1, count)]

    def scores(sl, left, right, lo):
        for n in range(2):
            cols = slice(n * 256, (n + 1) * 256)
            S[sl, :, cols] = lax.dot_general(
                left[...], right[lo + n * 256:lo + (n + 1) * 256, :], NT, preferred_element_type=f32)
        return soft(sl)

    def combine(buf, j, count):
        ms = [buf[j, r, 0:1, :] for r in range(count)]
        M = ms[0]
        for v in ms[1:]:
            M = jnp.maximum(M, v)
        L = jnp.zeros_like(M)
        for r in range(count):
            L = L + buf[j, r, 1:2, :] * jnp.exp2((ms[r] - M) * KAPPA)
        return jnp.exp2((ms[0] - M) * KAPPA) / L

    def wait_bytes(ref, sem):
        pltpu.make_async_copy(ref, ref, sem).wait()

    def weights(sl, f, rows):
        p = S[sl, rows, :] * f
        q = p[:, 0:128]
        for i in range(1, 4):
            q = q + p[:, i * 128:(i + 1) * 128]
        mass[rows, :] += q
        return p.astype(bf16)

    def A(j):
        at, sl = CHUNKS[j], j % SLOTS
        ready(at)
        ready(at + 256)
        m, l = scores(sl, ce, img, at)
        stat[j, 0, 0:1, :] = m
        stat[j, 0, 1:2, :] = l
        if j:
            send_stats(j)

    def send_stats(j):
        for cp in stat_copies(stat, j, 16, ss, sr, centpeer):
            cp.start()

    def B(j):
        at = CHUNKS[j]
        wait_bytes(stat.at[j, pl.ds(1, 15)], sr.at[j])
        f = combine(stat, j, 16)
        for t in range(0, ROWS, 512):
            rows = slice(t, t + 512)
            p = weights(j % SLOTS, f, rows)
            for d in range(3):
                cols = slice(d * 512, (d + 1) * 512)
                v = lax.dot_general(p, img[at:at + 512, cols], NN, preferred_element_type=f32)
                if j == 0:
                    acc[rows, cols] = v
                else:
                    acc[rows, cols] += v

    A(0)
    pl.semaphore_wait(barrier, len(everyone))
    start(*FIRST)
    send_stats(0)
    for l in l_to:
        l.start()
    for step in STEPS:
        if step[0] == "A":
            A(step[1])
        elif step[0] == "B":
            B(step[1])
        else:
            arrive(*relay[step][0])
            start(*relay[step][1])

    for t in range(0, ROWS, 256):
        rows = slice(t, t + 256)
        inv = 1.0 / (jnp.sum(mass[rows, :], axis=1, keepdims=True) + prior)
        data[rows, :] = ((acc[rows, :] + prior * ce[rows, :].astype(f32)) * inv).astype(bf16)
    o1 = pltpu.make_async_copy(data.at[pl.ds(pl.multiple_of(di * 128, 128), 128)], out1, ld.at[0])
    o1.start()

    for l in l_to:
        l.wait()
    mass[...] = jnp.zeros_like(mass)
    for h in range(2):
        m, l = scores(h, to, data, h * 512)
        stat2[h, 0, 0:1, :] = m
        stat2[h, 0, 1:2, :] = l
        for cp in stat_copies(stat2, h, 8, s2s, s2r, dppeer):
            cp.start()
    wait_bytes(stat2.at[0, pl.ds(1, 7)], s2r.at[0])
    f = combine(stat2, 0, 8)
    for t in range(0, ROWS, 512):
        rows = slice(t, t + 512)
        p = weights(0, f, rows)
        for d in range(3):
            cols = slice(d * 512, (d + 1) * 512)
            acc[rows, cols] = lax.dot_general(p, data[0:512, cols], NN, preferred_element_type=f32)
    wait_bytes(stat2.at[1, pl.ds(1, 7)], s2r.at[1])
    f = combine(stat2, 1, 8)
    for t in range(0, ROWS, 512):
        rows = slice(t, t + 512)
        Pb[rows, :] = weights(1, f, rows)
    pair = lax.div(y, 2)
    d_copies = []
    for i in range(2):
        half = pl.multiple_of((1 - pair if i == 0 else pair) * 256, 256)
        src = pl.ds(pl.multiple_of((1 - c) * 512 + half, 256), 256)
        for d in range(3):
            cols = slice(d * 512, (d + 1) * 512)
            v = acc[src, cols] + lax.dot_general(Pb[src, :], data[512:1024, cols], NN, preferred_element_type=f32)
            dsend[pl.ds(half, 256), cols] = v.astype(bf16)
        cp = pltpu.make_async_remote_copy(
            src_ref=dsend.at[pl.ds(half, 256)], dst_ref=drecv.at[pl.ds(half, 256)],
            send_sem=ds.at[i], recv_sem=dr.at[i], device_id=partner, device_id_type=MESH)
        cp.start()
        d_copies.append(cp)
    msum[0] = jnp.sum(mass[...].T, axis=0, keepdims=True)
    m_copies = [pltpu.make_async_remote_copy(
        src_ref=msum.at[0], dst_ref=msum.at[r], send_sem=mss, recv_sem=msr,
        device_id=centpeer(r), device_id_type=MESH) for r in range(1, 16)]
    for cp in m_copies:
        cp.start()

    blocks = []

    def send(i, src, dst, device):
        cp = pltpu.make_async_remote_copy(
            src_ref=src, dst_ref=dst, send_sem=rs.at[i], recv_sem=rr.at[i], device_id=device, device_id_type=MESH)
        cp.start()
        blocks.append(cp)
        return cp

    def at(yy, zz):
        return pl.ds(pl.multiple_of(c * 512 + yy * 128 + zz * 64, 64), 64)

    zpartner = dev(x, y, zh, 1 - zl, c)
    LEFT, RIGHT = slice(0, D // 2), slice(D // 2, D)
    first, along_y, along_z = {}, {}, {}
    for i in range(2):
        half = pl.multiple_of((1 - pair if i == 0 else pair) * 256, 256)
        src = pl.ds(pl.multiple_of(c * 512 + half, 256), 256)
        for d in range(3):
            cols = slice(d * 512, (d + 1) * 512)
            acc[src, cols] += lax.dot_general(Pb[src, :], data[512:1024, cols], NN, preferred_element_type=f32)
        d_copies[i].wait_recv()
        acc[src, :] += drecv[pl.ds(half, 256), :].astype(f32)
        for r in ((2, 3) if i == 0 else (1, 0)):
            yy = xor4(y, r)
            zs[r] = acc[at(yy, 1 - zl), RIGHT].astype(bf16)
            along_z[r] = send(r, zs.at[r], zr.at[r], zpartner)
            if r == 2:
                for h in range(2):
                    fs[h] = acc[at(yy, h), LEFT].astype(bf16)
                    first[h] = send(4 + 2 * h, fs.at[h], fr.at[h], dev(x, xor4(y, 1 + 2 * h), zh, zl, c))
    for r in (3, 1):
        yy = xor4(y, r)
        h = 0 if r == 3 else 1
        first[h].wait_recv()
        for zz in range(2):
            v = acc[at(yy, zz), LEFT]
            if zz == h:
                v = v + fr[h].astype(f32)
            ys[r, zz * 64:(zz + 1) * 64, :] = v.astype(bf16)
        along_y[r] = send(4 + r, ys.at[r], yr.at[r], dev(x, yy, zh, zl, c))
    along_y2 = {}
    for r in (2, 3, 1):
        yy = xor4(y, r)
        along_z[r].wait_recv()
        y2s[r] = (acc[at(yy, zl), RIGHT] + zr[r].astype(f32)).astype(bf16)
        along_y2[r] = send(8 + r, y2s.at[r], y2r.at[r], dev(x, yy, zh, zl, c))
    here = c * 512 + y * 128 + zl * 64
    wait_bytes(msum.at[pl.ds(1, 15)], msr)
    total = msum[0]
    for r in range(1, 16):
        total = total + msum[r]
    lane = lax.broadcasted_iota(jnp.int32, (64, ROWS), 1)
    sub = lax.broadcasted_iota(jnp.int32, (64, ROWS), 0)
    col = jnp.sum(jnp.where(lane == sub + here, total, 0.0), axis=1, keepdims=True)
    inv = 1.0 / (col + prior)
    for r in (3, 1):
        along_y[r].wait_recv()

    def left(zz):
        rows = pl.ds(pl.multiple_of(zz * 64, 64), 64)
        v = acc[at(y, zz), LEFT]
        for r in (1, 3):
            v = v + yr[r, rows, :].astype(f32)
        return v

    z2s[...] = left(1 - zl).astype(bf16)
    along_z2 = send(12, z2s, z2r, zpartner)
    own = left(zl) + prior * to[at(y, zl), LEFT].astype(f32)
    along_z[0].wait_recv()
    right = acc[at(y, zl), RIGHT] + prior * to[at(y, zl), RIGHT].astype(f32) + zr[0].astype(f32)
    for r in (2, 3, 1):
        along_y2[r].wait_recv()
        right = right + y2r[r].astype(f32)
    res[:, RIGHT] = (right * inv).astype(bf16)
    along_z2.wait_recv()
    res[:, LEFT] = ((own + z2r[...].astype(f32)) * inv).astype(bf16)
    o2 = pltpu.make_async_copy(res, out2, ld.at[1])
    o2.start()

    for cp in names.values():
        cp.wait_send()
    for j in range(8):
        wait_bytes(stat.at[j, pl.ds(1, 15)], ss.at[j])
    for h in range(2):
        wait_bytes(stat2.at[h, pl.ds(1, 7)], s2s.at[h])
    wait_bytes(msum.at[pl.ds(1, 15)], mss)
    for cp in d_copies + blocks:
        cp.wait_send()
    o1.wait()
    o2.wait()


def hand_over(a, b, out1, out2):
    out1[...] = a[...]
    out2[0] = b[...]


def body(images, cents, tops):
    anyspec = pl.BlockSpec(memory_space=pl.ANY)
    vmem = pl.BlockSpec(memory_space=pltpu.VMEM)
    ncopies = 108
    flops = 2 * 2 * (1024 * 4096 + 1024 * 1024) * D
    part, top = pl.pallas_call(
        kernel,
        out_shape=(jax.ShapeDtypeStruct((128, D), bf16), jax.ShapeDtypeStruct((64, D), bf16)),
        in_specs=[anyspec] * 3,
        out_specs=(anyspec, anyspec),
        scratch_shapes=[
            pltpu.VMEM((8 * SHARD, D), bf16),
            pltpu.VMEM((ROWS, D), bf16),
            pltpu.VMEM((ROWS, D), bf16),
            pltpu.VMEM((SLOTS, ROWS, 512), f32),
            pltpu.VMEM((ROWS, 512), bf16),
            pltpu.VMEM((ROWS, D), f32),
            pltpu.VMEM((ROWS, 128), f32),
            pltpu.VMEM((ROWS, D), bf16),
            pltpu.VMEM((8, 16, 2, 512), f32),
            pltpu.VMEM((2, 8, 2, 512), f32),
            pltpu.VMEM((16, 1, 1024), f32),
            pltpu.VMEM((512, D), bf16),
            pltpu.VMEM((512, D), bf16),
            pltpu.VMEM((4, 64, D // 2), bf16),
            pltpu.VMEM((4, 64, D // 2), bf16),
            pltpu.VMEM((2, 64, D // 2), bf16),
            pltpu.VMEM((2, 64, D // 2), bf16),
            pltpu.VMEM((4, 128, D // 2), bf16),
            pltpu.VMEM((4, 128, D // 2), bf16),
            pltpu.VMEM((4, 64, D // 2), bf16),
            pltpu.VMEM((4, 64, D // 2), bf16),
            pltpu.VMEM((64, D // 2), bf16),
            pltpu.VMEM((64, D // 2), bf16),
            pltpu.VMEM((64, D), bf16),
            pltpu.SemaphoreType.DMA((ncopies,)),
            pltpu.SemaphoreType.DMA((ncopies,)),
            pltpu.SemaphoreType.DMA((8,)),
            pltpu.SemaphoreType.DMA((8,)),
            pltpu.SemaphoreType.DMA((2,)),
            pltpu.SemaphoreType.DMA((2,)),
            pltpu.SemaphoreType.DMA,
            pltpu.SemaphoreType.DMA,
            pltpu.SemaphoreType.DMA((2,)),
            pltpu.SemaphoreType.DMA((2,)),
            pltpu.SemaphoreType.DMA((13,)),
            pltpu.SemaphoreType.DMA((13,)),
            pltpu.SemaphoreType.DMA((18,)),
        ],
        compiler_params=pltpu.CompilerParams(
            collective_id=0, has_side_effects=True, vmem_limit_bytes=60 * 1024 * 1024),
        cost_estimate=pl.CostEstimate(flops=flops, bytes_accessed=9 * 1024 * 1024, transcendentals=6 * 1024 * 1024),
        name="two_levels",
    )(images, cents, tops)
    return pl.pallas_call(
        hand_over,
        out_shape=(jax.ShapeDtypeStruct((128, D), bf16), jax.ShapeDtypeStruct((1, 64, D), bf16)),
        in_specs=[vmem] * 2,
        out_specs=(vmem, vmem),
        name="hand_over",
    )(part, top)


def solution(mesh):
    return jax.shard_map(
        body,
        mesh=mesh,
        in_specs=(P("dp", None), P("cent", None), P("dp", None)),
        out_specs=(P(("cent", "dp"), None), P("dp", "cent", None)),
        check_vma=False,
    )
```

```python
import jax
import jax.numpy as jnp
from jax import lax
from jax.experimental import pallas as pl
from jax.experimental.pallas import tpu as pltpu
from jax.sharding import PartitionSpec as P

prior = 0.1
MESH = pl.DeviceIdType.MESH
f32, bf16 = jnp.float32, jnp.bfloat16
NT = (((1,), (1,)), ((), ()))
NN = (((1,), (0,)), ((), ()))
D = 1536
SHARD = 512
ROWS = 1024
HX, HQ = 128, 32
LEFT_D = 640
KAPPA = D ** -0.5 * 1.4426950408889634
ORDER = (1, 3, 2)
AT_X = {(0, 1): 1024, (0, 3): 1152, (0, 2): 2048, (1, 1): 2560, (1, 3): 3072, (1, 2): 3584}
AT_Y = {(0, 1): 1536, (0, 3): 1792, (0, 2): 2304, (1, 1): 2816, (1, 3): 3328, (1, 2): 3840}
CHUNKS = (0, 1024, 512, 1536, 2048, 2560, 3072, 3584)
SLOTS = 4
FIRST = (
    ('xx', 1, 0), ('xx', 3, 0), ('xq', 0, 1), ('xq', 0, 3), ('zr', 0), ('zq',), ('zr', 1), ('zr', 2),
    ('zr', 3), ('xx', 1, 1), ('xx', 3, 1), ('xq', 0, 2),
)
SECOND = (
    ('xq', 1, 1), ('xq', 1, 3), ('xq', 1, 2), ('dzq',),
)
STEPS = (
    ('B', 0), ('xr', 1, 0), ('xr', 3, 0), ('zrs', 0), ('zqs',), ('yf', 0, 1), ('yf', 0, 3), ('zrs', 1),
    ('zrs', 2), ('zrs', 3), ('yr', 0, 1, 1), ('yr', 0, 1, 3), ('xr', 1, 1), ('xr', 3, 1), ('zis', 0),
    ('yr', 0, 3, 1), ('yr', 0, 3, 3), ('zis', 1), ('yf', 0, 2), ('yr', 0, 1, 2), ('A', 1), ('yf', 1, 1),
    ('l', 1, 0), ('zis', 2), ('zis', 3), ('yr', 0, 3, 2), ('l', 1, 1), ('xr', 2, 0), ('yr', 0, 2, 3),
    ('yr', 0, 2, 1), ('A', 2), ('yf', 1, 3), ('l', 3, 0), ('l', 3, 1), ('lis', 1, 0), ('yr', 1, 1, 1),
    ('yr', 1, 1, 3), ('A', 3), ('yf', 1, 2), ('xr', 2, 1), ('lis', 1, 1), ('yr', 0, 2, 2), ('B', 1),
    ('lis', 3, 0), ('yr', 1, 3, 1), ('yr', 1, 3, 3), ('A', 4), ('l', 2, 0), ('lis', 3, 1), ('yr', 1, 1, 2),
    ('B', 2), ('l', 2, 1), ('yr', 1, 3, 2), ('yr', 1, 2, 1), ('yr', 1, 2, 3), ('B', 3), ('lis', 2, 0),
    ('A', 5), ('lis', 2, 1), ('yr', 1, 2, 2), ('A', 6), ('A', 7), ('B', 4), ('B', 5), ('B', 6), ('B', 7),
)


def xor4(v, r):
    if r == 0:
        return v
    if r == 1:
        return v + 1 - 2 * lax.rem(v, 2)
    if r == 2:
        return lax.rem(v + 2, 4)
    return 3 - v


def flip(v, r):
    return 1 - v if r else v


def kernel(images, cents, tops, out1, out2,
           img, ce, to, S, Pb, acc, mass, data, stat, stat2, msum, dsend, drecv, zs, zr, fs, fr, ys, yr, y2s, y2r, z2s, z2r, res,
           gs, gr, ss, sr, s2s, s2r, mss, msr, ds, dr, rs, rr, ld):
    ci = lax.axis_index("cent")
    di = lax.axis_index("dp")
    y, zl, c = lax.div(ci, 4), lax.rem(lax.div(ci, 2), 2), lax.rem(ci, 2)
    x, zh = lax.div(di, 2), lax.rem(di, 2)

    def dev(x, y, zh, zl, c):
        return ((y * 2 + zl) * 2 + c, x * 2 + zh)

    def centpeer(r):
        return dev(x, xor4(y, r // 4), zh, flip(zl, (r // 2) % 2), flip(c, r % 2))

    def dppeer(r):
        return dev(xor4(x, r // 2), y, flip(zh, r % 2), zl, c)

    partner = centpeer(1)
    zpeer = dev(x, y, 1 - zh, 1 - zl, c)

    l_img = pltpu.make_async_copy(images, img.at[pl.ds(0, SHARD)], ld.at[0])
    l_ce = pltpu.make_async_copy(cents, ce, ld.at[1])
    l_img.start()
    l_ce.start()
    l_to = []
    for b in range(16):
        yy, zz, cc = b // 4, (b // 2) % 2, b % 2
        pos = cc * 512 + yy * 128 + zz * 64
        l_to.append(pltpu.make_async_copy(tops.at[pl.ds(b * 64, 64)], to.at[pl.ds(pos, 64)], ld.at[2 + b]))

    barrier = pltpu.get_barrier_semaphore()
    everyone = [centpeer(r) for r in range(1, 16)] + [dppeer(r) for r in range(1, 8)] + [zpeer]
    for p in everyone:
        pl.semaphore_signal(barrier, inc=1, device_id=p, device_id_type=MESH)

    names = {}

    def copy(name, src, dst, device):
        i = len(names)
        names[name] = pltpu.make_async_remote_copy(
            src_ref=src, dst_ref=dst, send_sem=gs.at[i], recv_sem=gr.at[i],
            device_id=device, device_id_type=MESH)

    def rq(at, q, core):
        return pl.ds(pl.multiple_of(at + q * 64 + core * HQ, 16), HQ)

    def rqh(at, q, core, h):
        return pl.ds(pl.multiple_of(at + q * 64 + core * HQ + h * 16, 16), 16)

    def rxh(at, core, h):
        return pl.ds(pl.multiple_of(at + core * HX + h * 64, 16), 64)

    def near_at(s, core, h):
        if s == 2:
            return AT_X[0, 2] + core * HX + h * 64
        return AT_X[0, s] + h * 256 + core * 64

    def near(s, core, h):
        return pl.ds(pl.multiple_of(near_at(s, core, h), 16), 64)

    zinner = centpeer(2)
    rows = rq(256, y, c)
    rows1 = rq(768, y, c)
    copy(("zq",), img.at[rows], img.at[rows1], zpeer)
    copy(("dzq",), img.at[rows1], img.at[rows1], partner)
    for k in range(4):
        def part(at, h):
            return rxh(at, c, h) if k == 0 else rqh(at + 256, xor4(y, k), c, h)
        copy(("zr", k), img.at[part(0, 1 - zl)], img.at[part(512, 1 - zl)], zpeer)
        copy(("zi", k), img.at[part(512, zl)], img.at[part(512, zl)], zinner)
        copy(("dzr", k), img.at[part(512, zl)], img.at[part(512, zl)], partner)
        copy(("dzi", k), img.at[part(512, 1 - zl)], img.at[part(512, 1 - zl)], partner)
    for s in ORDER:
        device = dev(xor4(x, s), y, zh, zl, c)
        for h in range(2):
            if s != 2:
                copy(("xx", s, h), img.at[rxh(0, c, h)], img.at[near(s, c, h)], device)
            copy(("dxx", s, h), img.at[near(s, c, h)], img.at[near(s, c, h)], partner)
        if s != 2:
            h = 0 if s == 1 else 1
            copy(("xf", s), img.at[near(s, c, h)], img.at[near(2, c, h)], dev(xor4(x, 4 - s), y, zh, zl, c))
        for g in range(2):
            def there(core, h):
                return pl.ds(pl.multiple_of(AT_X[1, s] + core * HX + h * 64 + g * 32, 16), 32)
            src = pl.ds(pl.multiple_of(near_at(s, c, 1 - zl) + g * 32, 16), 32)
            copy(("lr", s, g), img.at[src], img.at[there(c, 1 - zl)], zpeer)
            copy(("li", s, g), img.at[there(c, zl)], img.at[there(c, zl)], zinner)
            copy(("dlr", s, g), img.at[there(c, zl)], img.at[there(c, zl)], partner)
            copy(("dli", s, g), img.at[there(c, 1 - zl)], img.at[there(c, 1 - zl)], partner)
        for z in range(2):
            rows = rq(AT_Y[z, s], y, c)
            copy(("xq", z, s), img.at[rq(z * SHARD + 256, y, c)], img.at[rows], device)
            for r in (1, 3):
                copy(("yq", z, s, r), img.at[rows], img.at[rows], dev(x, xor4(y, r), zh, zl, c))
                there = rqh(AT_Y[z, s], xor4(y, r), c, 0 if r == 1 else 1)
                copy(("yh", z, s, r), img.at[there], img.at[there], dev(x, xor4(y, 4 - r), zh, zl, c))
            for r in range(4):
                there = rq(AT_Y[z, s], xor4(y, r), c)
                copy(("dq", z, s, r), img.at[there], img.at[there], partner)

    def start(*ns):
        for n in ns:
            names[n].start()

    here_now = set()

    def arrive(*ns):
        for n in ns:
            if n not in here_now:
                here_now.add(n)
                names[n].wait_recv()

    relay = {("zqs",): ([("zq",)], SECOND)}
    for k in range(4):
        relay["zrs", k] = ([("zr", k)], [("zi", k), ("dzr", k)])
        relay["zis", k] = ([("zi", k)], [("dzi", k)])
    for s in ORDER:
        for g in range(2):
            relay["l", s, g] = ([("lr", s, g)], [("li", s, g), ("dlr", s, g)])
            relay["lis", s, g] = ([("li", s, g)], [("dli", s, g)])
        if s == 2:
            relay["xr", 2, 0] = ([("xf", 1)], [("dxx", 2, 0)])
            relay["xr", 2, 1] = ([("xf", 1), ("xf", 3)], [("lr", 2, 0), ("lr", 2, 1), ("dxx", 2, 1)])
        else:
            relay["xr", s, 0] = ([("xx", s, 0)], ([("xf", s)] if s == 1 else []) + [("dxx", s, 0)])
            relay["xr", s, 1] = ([("xx", s, 0), ("xx", s, 1)],
                                 ([("xf", s)] if s == 3 else []) + [("lr", s, 0), ("lr", s, 1), ("dxx", s, 1)])
        for z in range(2):
            relay["yf", z, s] = ([("xq", z, s)], [("yq", z, s, 1), ("yq", z, s, 3), ("dq", z, s, 0)])
            for r in (1, 3):
                relay["yr", z, s, r] = ([("yq", z, s, r)], [("yh", z, s, r), ("dq", z, s, r)])
            relay["yr", z, s, 2] = ([("yh", z, s, 1), ("yh", z, s, 3)], [("dq", z, s, 2)])

    def ready(at):
        if at == 512:
            arrive(("dzr", 0), ("dzi", 0))
        if at == 768:
            arrive(("dzq",), *[(n, k) for n in ("dzr", "dzi") for k in range(1, 4)])
        if at in (1024, 1280):
            h = (at - 1024) // 256
            arrive(("dxx", 1, h), ("dxx", 3, h))
        elif at == AT_X[0, 2]:
            arrive(("dxx", 2, 0), ("dxx", 2, 1))
        for (z, s), a in AT_X.items():
            if z and at == a:
                arrive(*[(n, s, g) for n in ("dlr", "dli") for g in range(2)])
        for key, a in AT_Y.items():
            if at == a:
                arrive(*[("dq",) + key + (r,) for r in range(4)])

    l_img.wait()
    l_ce.wait()

    mass[...] = jnp.zeros_like(mass)

    def soft(sl):
        ms, ls = [], []
        for n in (slice(0, 256), slice(256, 512)):
            m = jnp.max(S[sl, :, n], axis=0, keepdims=True)
            l = jnp.zeros((8, 256), f32)
            for t in range(0, ROWS, 128):
                e = jnp.exp2((S[sl, t:t + 128, n] - m) * KAPPA)
                S[sl, t:t + 128, n] = e
                l = l + jnp.sum(e.reshape(16, 8, 256), axis=0)
            ms.append(m)
            ls.append(jnp.sum(l, axis=0, keepdims=True))
        return jnp.concatenate(ms, axis=1), jnp.concatenate(ls, axis=1)

    def stat_copies(buf, j, count, ssem, rsem, peer):
        return [pltpu.make_async_remote_copy(
            src_ref=buf.at[j, 0], dst_ref=buf.at[j, r], send_sem=ssem.at[j], recv_sem=rsem.at[j],
            device_id=peer(r), device_id_type=MESH) for r in range(1, count)]

    def dots(sl, left, right, lo):
        for n in range(2):
            cols = slice(n * 256, (n + 1) * 256)
            S[sl, :, cols] = lax.dot_general(
                left[...], right[lo + n * 256:lo + (n + 1) * 256, :], NT, preferred_element_type=f32)

    def scores(sl, left, right, lo):
        dots(sl, left, right, lo)
        return soft(sl)

    def combine(buf, j, count):
        ms = [buf[j, r, 0:1, :] for r in range(count)]
        M = ms[0]
        for v in ms[1:]:
            M = jnp.maximum(M, v)
        L = jnp.zeros_like(M)
        for r in range(count):
            L = L + buf[j, r, 1:2, :] * jnp.exp2((ms[r] - M) * KAPPA)
        return jnp.exp2((ms[0] - M) * KAPPA) / L

    def wait_bytes(ref, sem):
        pltpu.make_async_copy(ref, ref, sem).wait()

    def weights(sl, f, rows):
        p = S[sl, rows, :] * f
        q = p[:, 0:128]
        for i in range(1, 4):
            q = q + p[:, i * 128:(i + 1) * 128]
        mass[rows, :] += q
        return p.astype(bf16)

    def A(j):
        at, sl = CHUNKS[j], j % SLOTS
        ready(at)
        ready(at + 256)
        m, l = scores(sl, ce, img, at)
        stat[j, 0, 0:1, :] = m
        stat[j, 0, 1:2, :] = l
        if j:
            send_stats(j)

    def send_stats(j):
        for cp in stat_copies(stat, j, 16, ss, sr, centpeer):
            cp.start()

    def B(j):
        wait_bytes(stat.at[j, pl.ds(1, 15)], sr.at[j])
        weighted(j)

    def weighted(j):
        at = CHUNKS[j]
        f = combine(stat, j, 16)
        for t in range(0, ROWS, 512):
            rows = slice(t, t + 512)
            p = weights(j % SLOTS, f, rows)
            for d in range(3):
                cols = slice(d * 512, (d + 1) * 512)
                v = lax.dot_general(p, img[at:at + 512, cols], NN, preferred_element_type=f32)
                if j == 0:
                    acc[rows, cols] = v
                else:
                    acc[rows, cols] += v

    A(0)
    pl.semaphore_wait(barrier, len(everyone))
    start(*FIRST)
    send_stats(0)
    for l in l_to:
        l.start()
    for step in STEPS:
        if step[0] == "A":
            A(step[1])
        elif step[0] == "B":
            if step[1] == 7:
                for l in l_to:
                    l.wait()
            B(step[1])
        else:
            arrive(*relay[step][0])
            start(*relay[step][1])

    for t in range(0, ROWS, 256):
        rows = slice(t, t + 256)
        inv = 1.0 / (jnp.sum(mass[rows, :], axis=1, keepdims=True) + prior)
        data[rows, :] = ((acc[rows, :] + prior * ce[rows, :].astype(f32)) * inv).astype(bf16)

    mass[...] = jnp.zeros_like(mass)
    for h in range(2):
        m, l = scores(h, to, data, h * 512)
        stat2[h, 0, 0:1, :] = m
        stat2[h, 0, 1:2, :] = l
        for cp in stat_copies(stat2, h, 8, s2s, s2r, dppeer):
            cp.start()
    o1 = pltpu.make_async_copy(data.at[pl.ds(pl.multiple_of(di * 128, 128), 128)], out1, ld.at[0])
    o1.start()
    wait_bytes(stat2.at[0, pl.ds(1, 7)], s2r.at[0])
    f = combine(stat2, 0, 8)
    for t in range(0, ROWS, 512):
        rows = slice(t, t + 512)
        p = weights(0, f, rows)
        for d in range(3):
            cols = slice(d * 512, (d + 1) * 512)
            acc[rows, cols] = lax.dot_general(p, data[0:512, cols], NN, preferred_element_type=f32)
    wait_bytes(stat2.at[1, pl.ds(1, 7)], s2r.at[1])
    f = combine(stat2, 1, 8)
    for t in range(0, ROWS, 512):
        rows = slice(t, t + 512)
        Pb[rows, :] = weights(1, f, rows)
    pair = lax.div(y, 2)
    d_copies = []
    for i in range(2):
        half = pl.multiple_of((1 - pair if i == 0 else pair) * 256, 256)
        src = pl.ds(pl.multiple_of((1 - c) * 512 + half, 256), 256)
        for d in range(3):
            cols = slice(d * 512, (d + 1) * 512)
            v = acc[src, cols] + lax.dot_general(Pb[src, :], data[512:1024, cols], NN, preferred_element_type=f32)
            dsend[pl.ds(half, 256), cols] = v.astype(bf16)
        cp = pltpu.make_async_remote_copy(
            src_ref=dsend.at[pl.ds(half, 256)], dst_ref=drecv.at[pl.ds(half, 256)],
            send_sem=ds.at[i], recv_sem=dr.at[i], device_id=partner, device_id_type=MESH)
        cp.start()
        d_copies.append(cp)
    msum[0] = jnp.sum(mass[...].T, axis=0, keepdims=True)
    m_copies = [pltpu.make_async_remote_copy(
        src_ref=msum.at[0], dst_ref=msum.at[r], send_sem=mss, recv_sem=msr,
        device_id=centpeer(r), device_id_type=MESH) for r in range(1, 16)]
    for cp in m_copies:
        cp.start()

    blocks = []

    def send(i, src, dst, device):
        cp = pltpu.make_async_remote_copy(
            src_ref=src, dst_ref=dst, send_sem=rs.at[i], recv_sem=rr.at[i], device_id=device, device_id_type=MESH)
        cp.start()
        blocks.append(cp)
        return cp

    def at(yy, zz):
        return pl.ds(pl.multiple_of(c * 512 + yy * 128 + zz * 64, 64), 64)

    def total_of(yy, zz, cols):
        rows = pl.ds(pl.multiple_of(yy * 128 + zz * 64, 64), 64)
        return acc[at(yy, zz), cols] + drecv[rows, cols].astype(f32)

    zpartner = dev(x, y, zh, 1 - zl, c)
    LEFT, RIGHT = slice(0, LEFT_D), slice(LEFT_D, D)
    first, along_y, along_z = {}, {}, {}
    for i in range(2):
        half = pl.multiple_of((1 - pair if i == 0 else pair) * 256, 256)
        src = pl.ds(pl.multiple_of(c * 512 + half, 256), 256)
        for d in range(3):
            cols = slice(d * 512, (d + 1) * 512)
            acc[src, cols] += lax.dot_general(Pb[src, :], data[512:1024, cols], NN, preferred_element_type=f32)
        d_copies[i].wait_recv()
        for r in ((2, 3) if i == 0 else (1, 0)):
            yy = xor4(y, r)
            zs[r] = total_of(yy, 1 - zl, RIGHT).astype(bf16)
            along_z[r] = send(r, zs.at[r], zr.at[r], zpartner)
            if r == 2:
                for h in range(2):
                    fs[h] = total_of(yy, h, LEFT).astype(bf16)
                    first[h] = send(4 + 2 * h, fs.at[h], fr.at[h], dev(x, xor4(y, 1 + 2 * h), zh, zl, c))
    for r in (3, 1):
        yy = xor4(y, r)
        h = 0 if r == 3 else 1
        first[h].wait_recv()
        for zz in range(2):
            v = total_of(yy, zz, LEFT)
            if zz == h:
                v = v + fr[h].astype(f32)
            ys[r, zz * 64:(zz + 1) * 64, :] = v.astype(bf16)
        along_y[r] = send(4 + r, ys.at[r], yr.at[r], dev(x, yy, zh, zl, c))
    along_y2 = {}
    for r in (2, 3, 1):
        yy = xor4(y, r)
        along_z[r].wait_recv()
        y2s[r] = (total_of(yy, zl, RIGHT) + zr[r].astype(f32)).astype(bf16)
        along_y2[r] = send(8 + r, y2s.at[r], y2r.at[r], dev(x, yy, zh, zl, c))
    here = c * 512 + y * 128 + zl * 64
    wait_bytes(msum.at[pl.ds(1, 15)], msr)
    total = msum[0]
    for r in range(1, 16):
        total = total + msum[r]
    lane = lax.broadcasted_iota(jnp.int32, (64, ROWS), 1)
    sub = lax.broadcasted_iota(jnp.int32, (64, ROWS), 0)
    col = jnp.sum(jnp.where(lane == sub + here, total, 0.0), axis=1, keepdims=True)
    inv = 1.0 / (col + prior)
    for r in (3, 1):
        along_y[r].wait_recv()

    def left(zz):
        rows = pl.ds(pl.multiple_of(zz * 64, 64), 64)
        v = total_of(y, zz, LEFT)
        for r in (1, 3):
            v = v + yr[r, rows, :].astype(f32)
        return v

    z2s[...] = left(1 - zl).astype(bf16)
    along_z2 = send(12, z2s, z2r, zpartner)
    own = left(zl) + prior * to[at(y, zl), LEFT].astype(f32)
    along_z[0].wait_recv()
    right = total_of(y, zl, RIGHT) + prior * to[at(y, zl), RIGHT].astype(f32) + zr[0].astype(f32)
    for r in (2, 3, 1):
        along_y2[r].wait_recv()
        right = right + y2r[r].astype(f32)
    res[:, RIGHT] = (right * inv).astype(bf16)
    along_z2.wait_recv()
    res[:, LEFT] = ((own + z2r[...].astype(f32)) * inv).astype(bf16)
    o2 = pltpu.make_async_copy(res, out2, ld.at[1])
    o2.start()

    for cp in names.values():
        cp.wait_send()
    for j in range(8):
        wait_bytes(stat.at[j, pl.ds(1, 15)], ss.at[j])
    for h in range(2):
        wait_bytes(stat2.at[h, pl.ds(1, 7)], s2s.at[h])
    wait_bytes(msum.at[pl.ds(1, 15)], mss)
    for cp in d_copies + blocks:
        cp.wait_send()
    o1.wait()
    o2.wait()


def hand_over(a, b, out1, out2):
    out1[...] = a[...]
    out2[0] = b[...]


def body(images, cents, tops):
    anyspec = pl.BlockSpec(memory_space=pl.ANY)
    vmem = pl.BlockSpec(memory_space=pltpu.VMEM)
    ncopies = 108
    flops = 2 * 2 * (1024 * 4096 + 1024 * 1024) * D
    part, top = pl.pallas_call(
        kernel,
        out_shape=(jax.ShapeDtypeStruct((128, D), bf16), jax.ShapeDtypeStruct((64, D), bf16)),
        in_specs=[anyspec] * 3,
        out_specs=(anyspec, anyspec),
        scratch_shapes=[
            pltpu.VMEM((8 * SHARD, D), bf16),
            pltpu.VMEM((ROWS, D), bf16),
            pltpu.VMEM((ROWS, D), bf16),
            pltpu.VMEM((SLOTS, ROWS, 512), f32),
            pltpu.VMEM((ROWS, 512), bf16),
            pltpu.VMEM((ROWS, D), f32),
            pltpu.VMEM((ROWS, 128), f32),
            pltpu.VMEM((ROWS, D), bf16),
            pltpu.VMEM((8, 16, 2, 512), f32),
            pltpu.VMEM((2, 8, 2, 512), f32),
            pltpu.VMEM((16, 1, 1024), f32),
            pltpu.VMEM((512, D), bf16),
            pltpu.VMEM((512, D), bf16),
            pltpu.VMEM((4, 64, D - LEFT_D), bf16),
            pltpu.VMEM((4, 64, D - LEFT_D), bf16),
            pltpu.VMEM((2, 64, LEFT_D), bf16),
            pltpu.VMEM((2, 64, LEFT_D), bf16),
            pltpu.VMEM((4, 128, LEFT_D), bf16),
            pltpu.VMEM((4, 128, LEFT_D), bf16),
            pltpu.VMEM((4, 64, D - LEFT_D), bf16),
            pltpu.VMEM((4, 64, D - LEFT_D), bf16),
            pltpu.VMEM((64, LEFT_D), bf16),
            pltpu.VMEM((64, LEFT_D), bf16),
            pltpu.VMEM((64, D), bf16),
            pltpu.SemaphoreType.DMA((ncopies,)),
            pltpu.SemaphoreType.DMA((ncopies,)),
            pltpu.SemaphoreType.DMA((8,)),
            pltpu.SemaphoreType.DMA((8,)),
            pltpu.SemaphoreType.DMA((2,)),
            pltpu.SemaphoreType.DMA((2,)),
            pltpu.SemaphoreType.DMA,
            pltpu.SemaphoreType.DMA,
            pltpu.SemaphoreType.DMA((2,)),
            pltpu.SemaphoreType.DMA((2,)),
            pltpu.SemaphoreType.DMA((13,)),
            pltpu.SemaphoreType.DMA((13,)),
            pltpu.SemaphoreType.DMA((18,)),
        ],
        compiler_params=pltpu.CompilerParams(
            collective_id=0, has_side_effects=True, vmem_limit_bytes=60 * 1024 * 1024),
        cost_estimate=pl.CostEstimate(flops=flops, bytes_accessed=9 * 1024 * 1024, transcendentals=6 * 1024 * 1024),
        name="two_levels",
    )(images, cents, tops)
    return pl.pallas_call(
        hand_over,
        out_shape=(jax.ShapeDtypeStruct((128, D), bf16), jax.ShapeDtypeStruct((1, 64, D), bf16)),
        in_specs=[vmem] * 2,
        out_specs=(vmem, vmem),
        name="hand_over",
    )(part, top)


def solution(mesh):
    return jax.shard_map(
        body,
        mesh=mesh,
        in_specs=(P("dp", None), P("cent", None), P("dp", None)),
        out_specs=(P(("cent", "dp"), None), P("dp", "cent", None)),
        check_vma=False,
    )
```
